256 devices in a mesh: view: 16 (over y, x_lo, core), tm: 16 (over x_hi, z).
Axes of the slice: x: 4 (x_hi: 2, x_lo: 2; x = x_hi * 2 + x_lo), y: 4, z: 8, core: 2. Of those that a mesh axis runs over, the one named last changes fastest.
Arguments:
- frames_in: bfloat16 [16, 64, 48, 1536], P('view', 'tm'), may hold values from -6 to 6
- modulation: float32 [4, 1536], replicated, may hold values from -3 to 3
- gates: float32 [2, 1536], replicated, may hold values from 1.5 to 4
- qk_gain: float32 [4, 64], replicated, may hold values from 1 to 6
- view_qkv: bfloat16 [1536, 3072], P(None, 'view'), may hold values from -0.15625 to 0.15625
- view_out: bfloat16 [1024, 1536], P('view'), may hold values from -0.1875 to 0.1875
- time_qkv: bfloat16 [1536, 3072], P(None, 'view'), may hold values from -0.15625 to 0.15625
- time_out: bfloat16 [1024, 1536], P('view'), may hold values from -0.1875 to 0.1875
- window_start: int32 [64], P('tm'), may hold values from -4 to 60, as said below
Outputs:
- frames_out: bfloat16 [16, 64, 48, 1536], P('view', 'tm')
The draws below stay inside these ranges and needn't reach their ends.
Inputs may be any that keep to these rules, and one draw needn't show every extreme that they name: window_start[f] is f - 4 or f - 3; frame 0 takes the first, frame 64 - 1 the second.
All inputs are finite; a program needn't handle non-finite values.
Results may differ from the reference program's by a relative error of at most 0.035.
The reference program's roundings to bfloat16 on the way count: a program that leaves them out, or rounds other values in their place, can miss the bound.
Values may be sent and summed in bfloat16 or wider, within the bound.
No kernel may reach another device: no remote copies, remote signals or barrier semaphores. Data moves between devices by JAX's collectives and lax.ppermute only.
A program may use at most 128 MiB of HBM per device.

```python
import jax
import jax.numpy as jnp
from jax import lax

D = 1536
HEADS = 16
HS = 64
WIN = 8
TOK_DEV = 48
VIEWS = 16
FRAMES = 64


def draw_qk_gain(key, part):
    key = jax.random.fold_in(key, 11)
    return jax.random.uniform(key, (4, HS), jnp.float32, 1.0, 3.0)


def draw_window_start(key, part):
    key = jax.random.fold_in(key, 7)
    offset = jax.random.randint(key, (FRAMES,), 0, 2).astype(jnp.int32)
    offset = offset.at[0].set(0).at[FRAMES - 1].set(1)
    return (jnp.arange(FRAMES, dtype=jnp.int32) - WIN // 2 + offset).astype(jnp.int32)


def block_scale(key, extent, split, least, high):
    level = 1.0
    for dim, blocks in split:
        heights = jax.random.uniform(jax.random.fold_in(jax.random.fold_in(key, 6), dim), (blocks,), jnp.float32, least / len(split), high / len(split))
        level = level * jnp.repeat(jnp.exp(heights), extent[dim] // blocks).reshape((-1,) + (1,) * (len(extent) - 1 - dim))
    return level


def bell_draw(own_key, shape, scale, bound, split=(), kind=jnp.bfloat16):
    result = jax.random.normal(own_key, shape, jnp.float32) * scale
    if len(split) > 0:
        result = block_scale(own_key, shape, split, -0.22, 0.18) * result
    return jnp.clip(result, min=-bound, max=bound).astype(kind)


def setup_inputs(seed: int = 0) -> dict:
    arg_keys = jax.random.split(jax.random.key(seed), 10)
    return {
        "frames_in": bell_draw(arg_keys[0], (VIEWS, FRAMES, TOK_DEV, D), 1.0, 6.0, ((0, 16), (1, 16))),
        "modulation": bell_draw(arg_keys[1], (4, D), 0.5, 3.0, (), jnp.float32),
        "gates": jnp.clip(jax.random.uniform(arg_keys[2], (2, D), jnp.float32, 1.5, 4.0), 1.5, 4.0),
        "qk_gain": draw_qk_gain(jax.random.fold_in(arg_keys[9], 71), 0),
        "view_qkv": bell_draw(arg_keys[4], (D, HEADS * 3 * HS), D ** -0.5, 0.15625, ((1, 16),)),
        "view_out": bell_draw(arg_keys[5], (HEADS * HS, D), (HEADS * HS) ** -0.5, 0.1875, ((0, 16),)),
        "time_qkv": bell_draw(arg_keys[6], (D, HEADS * 3 * HS), D ** -0.5, 0.15625, ((1, 16),)),
        "time_out": bell_draw(arg_keys[7], (HEADS * HS, D), (HEADS * HS) ** -0.5, 0.1875, ((0, 16),)),
        "window_start": draw_window_start(jax.random.fold_in(arg_keys[9], 71), 0),
    }


EPSILON = 1e-06

def layer_norm(inputs, shift_vec, scale_vec):
    average = lax.optimization_barrier(jnp.mean(inputs, -1, keepdims=True))
    centred = inputs - average
    spread = lax.optimization_barrier(jnp.mean(centred * centred, -1, keepdims=True))
    return centred * lax.rsqrt(spread + EPSILON) * (1.0 + scale_vec) + shift_vec

def rms_norm(tensor_in, gain_row):
    values_f = tensor_in.astype(jnp.float32)
    square = lax.optimization_barrier(jnp.mean(values_f * values_f, -1, keepdims=True))
    return (values_f * lax.rsqrt(square + EPSILON) * gain_row).astype(jnp.bfloat16)

def masked_softmax(scores, allowed):
    scores = jnp.where(allowed, scores, -jnp.inf)
    largest = lax.optimization_barrier(jnp.max(scores, -1, keepdims=True))
    raised = jnp.where(allowed, jnp.exp(scores - largest), 0.0)
    return (raised / lax.optimization_barrier(jnp.sum(raised, -1, keepdims=True))).astype(jnp.bfloat16)

def project_split(normed, weight):
    flat = jnp.dot(normed.reshape(-1, D), weight, preferred_element_type=jnp.float32).astype(jnp.bfloat16)
    return flat.reshape(VIEWS, FRAMES, TOK_DEV, HEADS, 3, HS)

def reference(frames_in, modulation, gates, qk_gain, view_qkv, view_out, time_qkv, time_out, window_start):
    inputs = frames_in.astype(jnp.float32)
    scaling = HS ** (-0.5)
    normed0 = layer_norm(inputs, modulation[0], modulation[1]).astype(jnp.bfloat16)
    split0 = project_split(normed0, view_qkv)
    queries0 = rms_norm(split0[..., 0, :], qk_gain[0])
    key_rows0 = rms_norm(split0[..., 1, :], qk_gain[1])
    value_rows0 = split0[..., 2, :]

    def frame_attend(frame_block):
        query_f, key_f, value_f = frame_block
        query_f = query_f.reshape(VIEWS * TOK_DEV, HEADS, HS).astype(jnp.float32)
        key_f = key_f.reshape(VIEWS * TOK_DEV, HEADS, HS).astype(jnp.float32)
        value_f = value_f.reshape(VIEWS * TOK_DEV, HEADS, HS).astype(jnp.float32)
        scores = jnp.einsum('qhd,khd->hqk', query_f, key_f) * scaling
        weights = masked_softmax(scores, jnp.ones(scores.shape, dtype=bool))
        attended = jnp.einsum('hqk,khd->qhd', weights.astype(jnp.float32), value_f).astype(jnp.bfloat16)
        return attended.reshape(VIEWS, TOK_DEV, HEADS, HS)
    attended0 = lax.map(frame_attend, (queries0.transpose(1, 0, 2, 3, 4), key_rows0.transpose(1, 0, 2, 3, 4), value_rows0.transpose(1, 0, 2, 3, 4)))
    attended0 = attended0.transpose(1, 0, 2, 3, 4).reshape(-1, HEADS * HS)
    branch0 = jnp.dot(attended0, view_out, preferred_element_type=jnp.float32).reshape(inputs.shape)
    middle = (inputs + gates[0] * branch0).astype(jnp.bfloat16)
    normed1 = layer_norm(middle.astype(jnp.float32), modulation[2], modulation[3]).astype(jnp.bfloat16)
    split1 = project_split(normed1, time_qkv)
    queries1 = rms_norm(split1[..., 0, :], qk_gain[2]).astype(jnp.float32)
    key_rows1 = rms_norm(split1[..., 1, :], qk_gain[3]).astype(jnp.float32)
    value_rows1 = split1[..., 2, :].astype(jnp.float32)
    frame_ids = jnp.arange(FRAMES, dtype=jnp.int32)
    window_lo = window_start[:, None]
    allowed = (frame_ids[None, :] >= window_lo) & (frame_ids[None, :] < window_lo + WIN)
    scores1 = jnp.einsum('vftha,vgtha->vthfg', queries1, key_rows1) * scaling
    weights1 = masked_softmax(scores1, allowed)
    attended1 = jnp.einsum('vthfg,vgtha->vftha', weights1.astype(jnp.float32), value_rows1).astype(jnp.bfloat16)
    branch1 = jnp.dot(attended1.reshape(-1, HEADS * HS), time_out, preferred_element_type=jnp.float32)
    return (middle.astype(jnp.float32) + gates[1] * branch1.reshape(inputs.shape)).astype(jnp.bfloat16)
```

```python
import functools

import jax
import jax.numpy as jnp
from jax import lax
from jax.experimental import pallas as pl
from jax.experimental.pallas import tpu as pltpu
from jax.sharding import PartitionSpec as P

HS = 64
WIN = 8
EPSILON = 1e-06
GROUP = 4
LANES = GROUP * HS
BF = jnp.bfloat16
F32 = jnp.float32
NT = (((1,), (1,)), ((), ()))
VMEM_LIMIT = 56 * 1024 * 1024

Y, X, C = 4, 2, 2


def hop(value, dy=0, dx=0, dc=0):
    pairs = []
    for y in range(Y):
        for x in range(X):
            for c in range(C):
                source = (y * X + x) * C + c
                target = ((y + dy) % Y * X + (x ^ dx)) * C + (c ^ dc)
                pairs.append((source, target))
    return lax.ppermute(value, "view", pairs)


def layer_norm(inputs, shift_vec, scale_vec):
    average = jnp.mean(inputs, -1, keepdims=True)
    centred = inputs - average
    spread = jnp.mean(centred * centred, -1, keepdims=True)
    return centred * lax.rsqrt(spread + EPSILON) * (1.0 + scale_vec) + shift_vec


def head_sums():
    row = lax.broadcasted_iota(jnp.int32, (LANES, LANES), 0) // HS
    col = lax.broadcasted_iota(jnp.int32, (LANES, LANES), 1) // HS
    return (row == col).astype(F32).astype(BF)


def rms_norm(product, gain_row, ones):
    values = product.astype(BF).astype(F32)
    square = values * values
    upper = square.astype(BF)
    lower = (square - upper.astype(F32)).astype(BF)
    total = jnp.dot(upper, ones, preferred_element_type=F32)
    total = total + jnp.dot(lower, ones, preferred_element_type=F32)
    return values * lax.rsqrt(total * (1.0 / HS) + EPSILON) * gain_row


def attend(query, key, value, bias):
    lane = lax.broadcasted_iota(jnp.int32, query.shape, 1) // HS
    result = jnp.zeros(query.shape, F32)
    for head in range(GROUP):
        own = lane == head
        scores = lax.dot_general(
            jnp.where(own, query, 0.0).astype(BF), key, NT, preferred_element_type=F32
        )
        if bias is not None:
            scores = scores + bias
        largest = jnp.max(scores, -1, keepdims=True)
        raised = jnp.exp(scores - largest)
        weights = (raised * (1.0 / jnp.sum(raised, -1, keepdims=True))).astype(BF)
        product = jnp.dot(weights, value, preferred_element_type=F32)
        result = jnp.where(own, product, result)
    return result.astype(BF)


def norm_kernel(mod_ref, *refs):
    inputs, outs = refs[:-1], refs[-1]
    for place, ref in enumerate(inputs):
        outs[place] = layer_norm(ref[...].astype(F32), mod_ref[0:1], mod_ref[1:2]).astype(BF)


def norm_chunks(modulation, chunks):
    return pl.pallas_call(
        norm_kernel,
        out_shape=jax.ShapeDtypeStruct((len(chunks),) + chunks[0].shape, BF),
        compiler_params=pltpu.CompilerParams(vmem_limit_bytes=VMEM_LIMIT),
        cost_estimate=pl.CostEstimate(flops=10_000_000, bytes_accessed=2_000_000, transcendentals=0),
    )(modulation, *chunks)


def view_kernel(gain_ref, *refs):
    tokens, weights, (out_ref, h_ref, w_ref) = refs[:8], refs[8:12], refs[12:]
    rows = tokens[0].shape[0] * tokens[0].shape[1]
    for place, ref in enumerate(tokens):
        h_ref[place * rows : (place + 1) * rows, :] = ref[...].reshape(rows, ref.shape[-1])
    for part in range(3):
        for place, ref in enumerate(weights):
            w_ref[part, place * HS : (place + 1) * HS, :] = ref[part * HS : (part + 1) * HS, :]
    ones = head_sums()
    h = h_ref[...]
    query = lax.dot_general(h, w_ref[0], NT, preferred_element_type=F32)
    query = rms_norm(query, gain_ref[0:1] * HS ** (-0.5), ones)
    key = lax.dot_general(h, w_ref[1], NT, preferred_element_type=F32)
    key = rms_norm(key, gain_ref[1:2], ones).astype(BF)
    value = lax.dot_general(h, w_ref[2], NT, preferred_element_type=F32).astype(BF)
    out_ref[...] = attend(query, key, value, None).reshape(out_ref.shape)


def view_attention(gains, tokens, weights):
    pair, toks, width = tokens[0].shape
    total = 8 * pair * toks
    return pl.pallas_call(
        view_kernel,
        out_shape=jax.ShapeDtypeStruct((Y, total // Y, LANES), BF),
        scratch_shapes=[pltpu.VMEM((total, width), BF), pltpu.VMEM((3, LANES, width), BF)],
        compiler_params=pltpu.CompilerParams(vmem_limit_bytes=VMEM_LIMIT),
        cost_estimate=pl.CostEstimate(
            flops=4_000_000_000, bytes_accessed=6_000_000, transcendentals=2_400_000
        ),
    )(gains, *tokens, *weights)


def join_kernel(gate_ref, *refs):
    inputs, heads, pieces, out_ref = refs[:4], refs[4:8], refs[8:-1], refs[-1]
    total = jnp.zeros((heads[0].shape[0], out_ref.shape[-1]), F32)
    place = 0
    for core in range(C):
        for e in range(Y):
            column = core * X * HS
            for part in range(2 if e == 2 else 1):
                piece = pieces[place][...]
                place += 1
                total = total + jnp.dot(
                    heads[e][:, column : column + piece.shape[0]], piece, preferred_element_type=F32
                )
                column += piece.shape[0]
    total = (total * gate_ref[...]).reshape(out_ref.shape)
    for d in range(4):
        out_ref[d] = (inputs[d][...].astype(F32) + total[d]).astype(BF)


def join_heads(gate, inputs, heads, pieces):
    toks, width = inputs[0].shape
    return pl.pallas_call(
        join_kernel,
        out_shape=jax.ShapeDtypeStruct((4, toks, width), BF),
        compiler_params=pltpu.CompilerParams(vmem_limit_bytes=VMEM_LIMIT),
        cost_estimate=pl.CostEstimate(flops=600_000_000, bytes_accessed=5_000_000, transcendentals=0),
    )(gate, *inputs, *heads, *pieces)


def time_kernel(toks, place_ref, start_ref, gain_ref, mod_ref, gate_ref, *refs):
    blocks, rest = refs[:6], refs[6:]
    pieces, (out_ref, h_ref, w_ref, o_ref, sems) = rest[:-5], rest[-5:]
    copies = []
    head = 0
    order = []
    for ref in pieces:
        for part in range(ref.shape[0] // LANES):
            for kind in range(4):
                copy = pltpu.make_async_copy(
                    ref.at[pl.ds(part * LANES + kind * HS, HS), :],
                    w_ref.at[kind, pl.ds(head * HS, HS), :],
                    sems.at[head, kind],
                )
                copy.start()
                copies.append(copy)
            head += 1
    heads = head
    own = 4 * toks
    scale, shift = mod_ref[1:2], mod_ref[0:1]
    for d in range(4):
        h_ref[d * toks : (d + 1) * toks, :] = layer_norm(
            blocks[d][...].astype(F32), shift, scale
        ).astype(BF)
    for side in range(2):
        at = own * (1 + side)
        h_ref[at : at + own, :] = layer_norm(
            blocks[4 + side][...].reshape(own, -1).astype(F32), shift, scale
        ).astype(BF)
    place, first = place_ref[0], place_ref[1]
    row = lax.broadcasted_iota(jnp.int32, (own, 3 * own), 0)
    col = lax.broadcasted_iota(jnp.int32, (own, 3 * own), 1)
    row_slot, col_slot = row // toks, col // toks
    side = col_slot // 4
    frame = first + 4 * jnp.where(side == 1, -1, jnp.where(side == 2, 1, 0)) + ((col_slot % 4) ^ place)
    low = jnp.zeros((own, 3 * own), jnp.int32)
    for d in range(4):
        low = jnp.where(row_slot == d, start_ref[place ^ d], low)
    allowed = (row % toks == col % toks) & (frame >= low) & (frame < low + WIN)
    allowed = allowed & (frame >= 0) & (frame < place_ref[2])
    bias = jnp.where(allowed, 0.0, -1e30)
    ones = head_sums()
    for group in range(heads // GROUP):
        for copy in copies[group * GROUP * 4 : (group + 1) * GROUP * 4]:
            copy.wait()
        span = slice(group * LANES, (group + 1) * LANES)
        query = lax.dot_general(h_ref[:own, :], w_ref[0, span, :], NT, preferred_element_type=F32)
        query = rms_norm(query, gain_ref[0:1] * HS ** (-0.5), ones)
        key = lax.dot_general(h_ref[...], w_ref[1, span, :], NT, preferred_element_type=F32)
        key = rms_norm(key, gain_ref[1:2], ones).astype(BF)
        value = lax.dot_general(h_ref[...], w_ref[2, span, :], NT, preferred_element_type=F32).astype(BF)
        o_ref[:, span] = attend(query, key, value, bias)
    branch = jnp.dot(o_ref[...], w_ref[3], preferred_element_type=F32) * gate_ref[...]
    for d in range(4):
        out_ref[0, place ^ d] = (
            blocks[d][...].astype(F32) + branch[d * toks : (d + 1) * toks, :]
        ).astype(BF)


def time_attention(place, starts, gains, modulation, gate, blocks, pieces):
    toks, width = blocks[0].shape
    own = 4 * toks
    heads = sum(piece.shape[0] for piece in pieces) // LANES
    smem = pl.BlockSpec(memory_space=pltpu.SMEM)
    vmem = pl.BlockSpec(memory_space=pltpu.VMEM)
    return pl.pallas_call(
        functools.partial(time_kernel, toks),
        out_shape=jax.ShapeDtypeStruct((1, 4, toks, width), BF),
        in_specs=[smem, smem, vmem, vmem, vmem]
        + [vmem] * len(blocks)
        + [pl.BlockSpec(memory_space=pl.ANY)] * len(pieces),
        out_specs=vmem,
        scratch_shapes=[
            pltpu.VMEM((3 * own, width), BF),
            pltpu.VMEM((4, heads * HS, width), BF),
            pltpu.VMEM((own, heads * HS), BF),
            pltpu.SemaphoreType.DMA((heads, 4)),
        ],
        compiler_params=pltpu.CompilerParams(vmem_limit_bytes=VMEM_LIMIT),
        cost_estimate=pl.CostEstimate(
            flops=8_000_000_000, bytes_accessed=16_000_000, transcendentals=1_800_000
        ),
    )(place, starts, gains, modulation, gate, *blocks, *pieces)


def ring_gather(first, second):
    rows = first.shape[0]
    both = jnp.concatenate([first, second], 0)
    back = hop(both, dy=1)
    ahead = hop(both, dy=-1)
    far_first = hop(back[:rows], dy=1)
    far_second = hop(ahead[rows:], dy=-1)
    return both, ahead, far_first, far_second, back


def gather_pieces(piece):
    mine = ring_gather(piece, hop(piece, dx=1))
    return mine + tuple(hop(part, dc=1) for part in mine)


def on_device(
    frames_in, modulation, gates, qk_gain, view_qkv, view_out, time_qkv, time_out, window_start
):
    count, toks, width = frames_in.shape[1:]
    view = lax.axis_index("view")
    p = view % 4
    t = lax.axis_index("tm")
    steps = lax.axis_size("tm")
    gains = jnp.tile(qk_gain, (1, GROUP))

    def frame(d):
        return lax.dynamic_index_in_dim(frames_in[0], p ^ d, 0, keepdims=False)

    raw = [frame(0)] + [hop(frame(d), dx=d // 2, dc=d % 2) for d in (1, 2, 3)]
    first = norm_chunks(modulation[0:2], raw[:2])
    second = norm_chunks(modulation[0:2], raw[2:])

    w_own = view_qkv.T
    w_x = hop(w_own, dx=1)
    heads_w = [w_own, w_x, hop(w_own, dc=1), hop(w_x, dc=1)]

    back_a, back_b = hop(first, dy=1), hop(second, dy=1)
    ahead_a, ahead_b = hop(first, dy=-1), hop(second, dy=-1)
    far_a, far_b = hop(back_a, dy=1), hop(ahead_b, dy=-1)
    tokens = [first, second, ahead_a, ahead_b, far_a, far_b, back_a, back_b]
    attended = view_attention(gains[0:2], tokens, heads_w)
    heads0 = [attended[0]] + [hop(attended[Y - e], dy=-e) for e in (1, 2, 3)]
    pieces0 = gather_pieces(view_out)
    middle = join_heads(gates[0:1], raw, heads0, pieces0)

    home = [middle[0]] + [hop(middle[d], dx=d // 2, dc=d % 2) for d in (1, 2, 3)]
    stacked = jnp.stack(home)
    up = [(i, i + 1) for i in range(steps - 1)]
    before = lax.ppermute(stacked, "tm", up)
    after = lax.ppermute(stacked, "tm", [(j, i) for i, j in up])

    pieces1 = gather_pieces(jnp.concatenate([time_qkv.T, time_out], 0))
    place = jnp.stack([p, t * count, steps * count]).astype(jnp.int32)
    return time_attention(
        place, window_start, gains[2:4], modulation[2:4], gates[1:2], home + [before, after], pieces1
    )


def solution(mesh):
    return jax.shard_map(
        on_device,
        mesh=mesh,
        in_specs=(
            P("view", "tm", None, None),
            P(),
            P(),
            P(),
            P(None, "view"),
            P("view", None),
            P(None, "view"),
            P("view", None),
            P("tm"),
        ),
        out_specs=P("view", "tm", None, None),
        check_vma=False,
    )
```

```python
import functools

import jax
import jax.numpy as jnp
from jax import lax
from jax.experimental import pallas as pl
from jax.experimental.pallas import tpu as pltpu
from jax.sharding import PartitionSpec as P

HS = 64
WIN = 8
EPSILON = 1e-06
GROUP = 4
LANES = GROUP * HS
BF = jnp.bfloat16
F32 = jnp.float32
NT = (((1,), (1,)), ((), ()))
VMEM_LIMIT = 56 * 1024 * 1024

Y, X, C = 4, 2, 2


def hop(value, dy=0, dx=0, dc=0, far=False):
    if far:
        steps = lax.axis_size("tm")
        pairs = []
        for view in range(Y * X * C):
            for step in range(steps):
                target = (view ^ C) * steps + (step + steps // 2) % steps
                pairs.append((view * steps + step, target))
        return lax.ppermute(value, ("view", "tm"), pairs)
    pairs = []
    for y in range(Y):
        for x in range(X):
            for c in range(C):
                source = (y * X + x) * C + c
                target = ((y + dy) % Y * X + (x ^ dx)) * C + (c ^ dc)
                pairs.append((source, target))
    return lax.ppermute(value, "view", pairs)


def fence(*values):
    return lax.optimization_barrier(values)


def layer_norm(inputs, shift_vec, scale_vec):
    average = jnp.mean(inputs, -1, keepdims=True)
    centred = inputs - average
    spread = jnp.mean(centred * centred, -1, keepdims=True)
    return centred * lax.rsqrt(spread + EPSILON) * (1.0 + scale_vec) + shift_vec


def head_sums():
    row = lax.broadcasted_iota(jnp.int32, (LANES, LANES), 0) // HS
    col = lax.broadcasted_iota(jnp.int32, (LANES, LANES), 1) // HS
    return (row == col).astype(F32).astype(BF)


def rms_norm(product, gain_row, ones):
    values = product.astype(BF).astype(F32)
    square = values * values
    upper = square.astype(BF)
    lower = (square - upper.astype(F32)).astype(BF)
    total = jnp.dot(upper, ones, preferred_element_type=F32)
    total = total + jnp.dot(lower, ones, preferred_element_type=F32)
    return values * lax.rsqrt(total * (1.0 / HS) + EPSILON) * gain_row


def attend(query, key, value, bias, stack):
    rows = query.shape[0]
    lane = lax.broadcasted_iota(jnp.int32, query.shape, 1) // HS
    result = jnp.zeros(query.shape, F32)
    for start in range(0, GROUP, stack):
        heads = range(start, start + stack)
        stacked = [jnp.where(lane == head, query, 0.0).astype(BF) for head in heads]
        stacked = jnp.concatenate(stacked, 0) if stack > 1 else stacked[0]
        scores = lax.dot_general(stacked, key, NT, preferred_element_type=F32)
        if bias is not None:
            scores = (scores.reshape(stack, rows, -1) + bias).reshape(stack * rows, -1)
        largest = jnp.max(scores, -1, keepdims=True)
        raised = jnp.exp(scores - largest)
        weights = (raised * (1.0 / jnp.sum(raised, -1, keepdims=True))).astype(BF)
        product = jnp.dot(weights, value, preferred_element_type=F32)
        for place, head in enumerate(heads):
            result = jnp.where(lane == head, product[place * rows : (place + 1) * rows], result)
    return result.astype(BF)


def norm_kernel(mod_ref, one_ref, other_ref, out_ref):
    for place, ref in enumerate((one_ref, other_ref)):
        out_ref[place] = layer_norm(ref[0].astype(F32), mod_ref[0:1], mod_ref[1:2]).astype(BF)


def norm_frames(modulation, one, other):
    shape = one.shape[1:]
    first = pl.BlockSpec((1,) + shape, lambda i: (0, 0, 0))
    second = pl.BlockSpec((1,) + shape, lambda i: (other.shape[0] - 1, 0, 0))
    if one is not other:
        second = first
    return pl.pallas_call(
        norm_kernel,
        grid=(1,),
        out_shape=jax.ShapeDtypeStruct((2,) + shape, BF),
        in_specs=[pl.BlockSpec(modulation.shape, lambda i: (0, 0)), first, second],
        out_specs=pl.BlockSpec((2,) + shape, lambda i: (0, 0, 0)),
        compiler_params=pltpu.CompilerParams(vmem_limit_bytes=VMEM_LIMIT),
        cost_estimate=pl.CostEstimate(flops=1_000_000, bytes_accessed=100_000, transcendentals=0),
    )(modulation, one, other)


def view_kernel(gain_ref, *refs):
    tokens, weights, (out_ref, h_ref, w_ref) = refs[:8], refs[8:12], refs[12:]
    rows = tokens[0].shape[0] * tokens[0].shape[1]
    for place, ref in enumerate(tokens):
        h_ref[place * rows : (place + 1) * rows, :] = ref[...].reshape(rows, ref.shape[-1])
    for part in range(3):
        for place, ref in enumerate(weights):
            w_ref[part, place * HS : (place + 1) * HS, :] = ref[part * HS : (part + 1) * HS, :]
    ones = head_sums()
    h = h_ref[...]
    query = lax.dot_general(h, w_ref[0], NT, preferred_element_type=F32)
    query = rms_norm(query, gain_ref[0:1] * HS ** (-0.5), ones)
    key = lax.dot_general(h, w_ref[1], NT, preferred_element_type=F32)
    key = rms_norm(key, gain_ref[1:2], ones).astype(BF)
    value = lax.dot_general(h, w_ref[2], NT, preferred_element_type=F32).astype(BF)
    out_ref[...] = attend(query, key, value, None, 1).reshape(out_ref.shape)


def view_attention(gains, tokens, weights):
    pair, toks, width = tokens[0].shape
    total = 8 * pair * toks
    return pl.pallas_call(
        view_kernel,
        out_shape=jax.ShapeDtypeStruct((Y, total // Y, LANES), BF),
        scratch_shapes=[pltpu.VMEM((total, width), BF), pltpu.VMEM((3, LANES, width), BF)],
        compiler_params=pltpu.CompilerParams(vmem_limit_bytes=VMEM_LIMIT),
        cost_estimate=pl.CostEstimate(
            flops=1_000_000, bytes_accessed=100_000, transcendentals=0
        ),
    )(gains, *tokens, *weights)


def join_kernel(gate_ref, mod_ref, keep_ref, got_ref, beside_ref, *refs):
    heads, pieces, outs, weight_ref = refs[:4], refs[4:8], refs[8:12], refs[12]
    for e in range(Y):
        for d, ref in enumerate(pieces):
            at = e * LANES + d * HS
            weight_ref[at : at + HS, :] = ref[e * HS : (e + 1) * HS, :]
    total = jnp.zeros((heads[0].shape[0], weight_ref.shape[-1]), F32)
    for e in range(Y):
        weight = weight_ref[e * LANES : (e + 1) * LANES, :]
        total = total + jnp.dot(heads[e][...], weight, preferred_element_type=F32)
    total = (total * gate_ref[0:1]).reshape((4,) + keep_ref.shape[1:])
    inputs = [keep_ref[0], got_ref[0], beside_ref[0], beside_ref[1]]
    for d in range(4):
        middle = (inputs[d].astype(F32) + total[d]).astype(BF)
        outs[d % 2][d // 2] = middle
        normed = layer_norm(middle.astype(F32), mod_ref[2:3], mod_ref[3:4])
        outs[2 + d % 2][d // 2] = normed.astype(BF)


def join_heads(gate, modulation, inputs, heads, pieces):
    pair, toks, width = inputs[0].shape
    return pl.pallas_call(
        join_kernel,
        out_shape=[jax.ShapeDtypeStruct((2, toks, width), BF)] * 4,
        scratch_shapes=[pltpu.VMEM((Y * LANES, width), BF)],
        compiler_params=pltpu.CompilerParams(vmem_limit_bytes=VMEM_LIMIT),
        cost_estimate=pl.CostEstimate(flops=1_000_000, bytes_accessed=100_000, transcendentals=0),
    )(gate, modulation, *inputs, *heads, *pieces)


def time_kernel(last, toks, place_ref, gain_ref, gate_ref, bias_ref, *refs):
    blocks, rest = refs[:3], refs[3:]
    extra, rest = (rest[:4], rest[4:]) if last else ((), rest)
    pieces, (out_ref, h_ref, w_ref, o_ref, sems) = rest[:-5], rest[-5:]
    own = 4 * toks
    copies = []
    head = 0
    for piece in pieces:
        for part in range(piece.shape[0] // LANES):
            for kind in range(4):
                copy = pltpu.make_async_copy(
                    piece.at[pl.ds(part * LANES + kind * HS, HS), :],
                    w_ref.at[kind, pl.ds(head * HS, HS), :],
                    sems.at[head, kind],
                )
                copy.start()
                copies.append(copy)
            head += 1
    for place, ref in enumerate(blocks):
        h_ref[place * own : (place + 1) * own, :] = ref[...].reshape(own, h_ref.shape[-1])
    ones = head_sums()
    for group in range(head // GROUP):
        for copy in copies[group * GROUP * 4 : (group + 1) * GROUP * 4]:
            copy.wait()
        span = slice(group * LANES, (group + 1) * LANES)
        query = lax.dot_general(h_ref[:own, :], w_ref[0, span, :], NT, preferred_element_type=F32)
        query = rms_norm(query, gain_ref[2:3] * HS ** (-0.5), ones)
        key = lax.dot_general(h_ref[...], w_ref[1, span, :], NT, preferred_element_type=F32)
        key = rms_norm(key, gain_ref[3:4], ones).astype(BF)
        value = lax.dot_general(h_ref[...], w_ref[2, span, :], NT, preferred_element_type=F32).astype(BF)
        o_ref[:, span] = attend(query, key, value, bias_ref[...], GROUP)
    branch = jnp.dot(o_ref[...], w_ref[3], preferred_element_type=F32)
    if not last:
        out_ref[...] = branch
        return
    partial_ref, even_ref, got_ref, beside_ref = extra
    branch = (branch + partial_ref[...]) * gate_ref[1:2]
    place = place_ref[0]
    middle = [even_ref[0], got_ref[0], beside_ref[0], beside_ref[1]]
    for d in range(4):
        rows = branch[d * toks : (d + 1) * toks, :]
        out_ref[0, place ^ d] = (middle[d].astype(F32) + rows).astype(BF)


def time_attention(place, gains, gates, bias, blocks, pieces, extra=()):
    count, toks, width = blocks[0].shape
    own = count * toks
    heads = sum(piece.shape[0] for piece in pieces) // LANES
    vmem = pl.BlockSpec(memory_space=pltpu.VMEM)
    out_shape = jax.ShapeDtypeStruct((own, width), F32)
    if extra:
        out_shape = jax.ShapeDtypeStruct((1, count, toks, width), BF)
    return pl.pallas_call(
        functools.partial(time_kernel, bool(extra), toks),
        out_shape=out_shape,
        in_specs=[pl.BlockSpec(memory_space=pltpu.SMEM)]
        + [vmem] * (3 + len(blocks) + len(extra))
        + [pl.BlockSpec(memory_space=pl.ANY)] * len(pieces),
        out_specs=vmem,
        scratch_shapes=[
            pltpu.VMEM((3 * own, width), BF),
            pltpu.VMEM((4, heads * HS, width), BF),
            pltpu.VMEM((own, heads * HS), BF),
            pltpu.SemaphoreType.DMA((heads, 4)),
        ],
        compiler_params=pltpu.CompilerParams(vmem_limit_bytes=VMEM_LIMIT),
        cost_estimate=pl.CostEstimate(
            flops=1_000_000, bytes_accessed=100_000, transcendentals=0
        ),
    )(place, gains, gates, bias, *blocks, *extra, *pieces)


def window_bias(place, first, frames, starts, toks):
    slots = jnp.arange(4, dtype=jnp.int32) ^ place
    low = starts[slots]
    frame = (first + 4 * jnp.array([0, -1, 1], jnp.int32)[:, None] + slots[None, :]).reshape(-1)
    allowed = (frame[None, :] >= low[:, None]) & (frame[None, :] < low[:, None] + WIN)
    allowed = allowed & (frame >= 0)[None, :] & (frame < frames)[None, :]
    same = jnp.eye(toks, dtype=bool)
    allowed = allowed[:, None, :, None] & same[None, :, None, :]
    return jnp.where(allowed, 0.0, -1e30).astype(F32).reshape(4 * toks, 12 * toks)


def on_device(
    frames_in, modulation, gates, qk_gain, view_qkv, view_out, time_qkv, time_out, window_start
):
    count, toks, width = frames_in.shape[1:]
    view = lax.axis_index("view")
    p = view % 4
    t = lax.axis_index("tm")
    steps = lax.axis_size("tm")
    gains = jnp.tile(qk_gain, (1, GROUP))

    def frames(*places):
        return jnp.stack(
            [lax.dynamic_index_in_dim(frames_in[0], p ^ d, 0, keepdims=False) for d in places]
        )

    parts = [view_out, hop(view_out, dy=-1), hop(view_out, dy=2), hop(view_out, dy=1)]

    keep, give = frames(0, 2), frames(1, 3)
    got = hop(give, dc=1)
    beside = hop(jnp.stack([keep[1], got[1]]), dx=1)
    first = norm_frames(modulation, keep, got)
    second = norm_frames(modulation, beside, beside)
    first, parts = fence(first, parts)
    back_a, ahead_a = hop(first, dy=1), hop(first, dy=-1)
    second, w_own = fence(second, view_qkv.T)
    w_x = hop(w_own, far=True)
    back_b, ahead_b = hop(second, dy=1), hop(second, dy=-1)
    far_a, far_b = hop(back_a, dy=1), hop(ahead_b, dy=-1)
    tokens = [first, second, ahead_a, ahead_b, far_a, far_b, back_a, back_b]
    heads_w = [w_own, hop(w_own, dc=1), w_x, hop(w_x, dc=1)]
    column = jnp.concatenate(fence(parts, ahead_a, back_a)[0], 0)
    column_x = hop(column, dx=1)
    time_own = jnp.concatenate([time_qkv.T, time_out], 0)
    tokens, heads_w, column, column_x, time_own = fence(
        tokens, heads_w, column, column_x, time_own
    )

    pieces0 = [column, hop(column, dc=1), column_x, hop(column_x, dc=1)]
    time_x = hop(time_own, far=True)
    attended = view_attention(gains, tokens, heads_w)
    attended, pieces0 = fence(attended, pieces0)
    heads0 = [attended[0]] + [hop(attended[Y - e], dy=-e) for e in (1, 2, 3)]
    time_x, heads0[0] = fence(time_x, heads0[0])
    pair_w = jnp.concatenate([time_own, time_x], 0)
    heads0, pair_w = fence(heads0, pair_w)
    back_w, ahead_w = hop(pair_w, dy=1), hop(pair_w, dy=-1)
    even, odd, even_h, odd_h = join_heads(gates, modulation, [keep, got, beside], heads0, pieces0)

    got_h = hop(odd_h, dc=1)
    beside_h = hop(jnp.stack([even_h[1], got_h[1]]), dx=1)
    home = jnp.concatenate([even_h[:1], got_h[:1], beside_h], 0)
    home, odd, pair_w = fence(home, odd, pair_w)
    up = [(i, i + 1) for i in range(steps - 1)]
    before = lax.ppermute(home, "tm", up)
    behind = lax.ppermute(home, "tm", [(j, i) for i, j in up])
    pair_c = hop(pair_w, dc=1)
    got_m = hop(odd, dc=1)
    beside_m = hop(jnp.stack([even[1], got_m[1]]), dx=1)
    bias = window_bias(p, t * count, steps * count, window_start, toks)
    before, behind, back_w, ahead_w, pair_c, bias = fence(
        before, behind, back_w, ahead_w, pair_c, bias
    )
    rows = time_own.shape[0]
    far = [hop(back_w[:rows], dy=1), hop(ahead_w[rows:], dy=-1)]
    sides = [ahead_w, back_w]
    pieces1 = [pair_w, pair_c] + sides + [hop(side, dc=1) for side in sides]
    place, blocks = p[None], [home, before, behind]
    partial = time_attention(place, gains, gates, bias, blocks, pieces1)
    partial, far, beside_m = fence(partial, far, beside_m)
    pieces2 = far + [hop(half, dc=1) for half in far]
    extra = [partial, even, got_m, beside_m]
    return time_attention(place, gains, gates, bias, blocks, pieces2, extra)


def solution(mesh):
    return jax.shard_map(
        on_device,
        mesh=mesh,
        in_specs=(
            P("view", "tm", None, None),
            P(),
            P(),
            P(),
            P(None, "view"),
            P("view", None),
            P(None, "view"),
            P("view", None),
            P("tm"),
        ),
        out_specs=P("view", "tm", None, None),
        check_vma=False,
    )
```

```python
import functools

import jax
import jax.numpy as jnp
from jax import lax
from jax.experimental import pallas as pl
from jax.experimental.pallas import tpu as pltpu
from jax.sharding import PartitionSpec as P

HS = 64
WIN = 8
EPSILON = 1e-06
GROUP = 4
STRIP = 16
LANES = GROUP * HS
BF = jnp.bfloat16
F32 = jnp.float32
NT = (((1,), (1,)), ((), ()))
VMEM_LIMIT = 56 * 1024 * 1024

Y, X, C = 4, 2, 2


def hop(value, dy=0, dx=0, dc=0, far=False):
    if far:
        steps = lax.axis_size("tm")
        pairs = []
        for view in range(Y * X * C):
            for step in range(steps):
                target = (view ^ C) * steps + (step + steps // 2) % steps
                pairs.append((view * steps + step, target))
        return lax.ppermute(value, ("view", "tm"), pairs)
    pairs = []
    for y in range(Y):
        for x in range(X):
            for c in range(C):
                source = (y * X + x) * C + c
                target = ((y + dy) % Y * X + (x ^ dx)) * C + (c ^ dc)
                pairs.append((source, target))
    return lax.ppermute(value, "view", pairs)


def fence(*values):
    return lax.optimization_barrier(values)


def layer_norm(inputs, shift_vec, scale_vec):
    average = jnp.mean(inputs, -1, keepdims=True)
    centred = inputs - average
    spread = jnp.mean(centred * centred, -1, keepdims=True)
    return centred * lax.rsqrt(spread + EPSILON) * (1.0 + scale_vec) + shift_vec


def head_sums():
    row = lax.broadcasted_iota(jnp.int32, (LANES, LANES), 0) // HS
    col = lax.broadcasted_iota(jnp.int32, (LANES, LANES), 1) // HS
    return (row == col).astype(F32).astype(BF)


def rms_norm(product, gain_row, ones):
    values = product.astype(BF).astype(F32)
    square = values * values
    upper = square.astype(BF)
    lower = (square - upper.astype(F32)).astype(BF)
    total = jnp.dot(upper, ones, preferred_element_type=F32)
    total = total + jnp.dot(lower, ones, preferred_element_type=F32)
    return values * lax.rsqrt(total * (1.0 / HS) + EPSILON) * gain_row


def attend(query, key, value, bias, stack):
    rows = query.shape[0]
    lane = lax.broadcasted_iota(jnp.int32, query.shape, 1) // HS
    result = jnp.zeros(query.shape, F32)
    for start in range(0, GROUP, stack):
        heads = range(start, start + stack)
        stacked = [jnp.where(lane == head, query, 0.0).astype(BF) for head in heads]
        stacked = jnp.concatenate(stacked, 0) if stack > 1 else stacked[0]
        scores = lax.dot_general(stacked, key, NT, preferred_element_type=F32)
        if bias is not None:
            scores = (scores.reshape(stack, rows, -1) + bias).reshape(stack * rows, -1)
        largest = jnp.max(scores, -1, keepdims=True)
        raised = jnp.exp(scores - largest)
        weights = (raised * (1.0 / jnp.sum(raised, -1, keepdims=True))).astype(BF)
        product = jnp.dot(weights, value, preferred_element_type=F32)
        for place, head in enumerate(heads):
            result = jnp.where(lane == head, product[place * rows : (place + 1) * rows], result)
    return result.astype(BF)


def norm_kernel(mod_ref, one_ref, other_ref, out_ref):
    for place, ref in enumerate((one_ref, other_ref)):
        out_ref[place] = layer_norm(ref[0].astype(F32), mod_ref[0:1], mod_ref[1:2]).astype(BF)


def norm_frames(modulation, one, other):
    shape = one.shape[1:]
    first = pl.BlockSpec((1,) + shape, lambda i: (0, 0, 0))
    second = pl.BlockSpec((1,) + shape, lambda i: (other.shape[0] - 1, 0, 0))
    if one is not other:
        second = first
    return pl.pallas_call(
        norm_kernel,
        grid=(1,),
        out_shape=jax.ShapeDtypeStruct((2,) + shape, BF),
        in_specs=[pl.BlockSpec(modulation.shape, lambda i: (0, 0)), first, second],
        out_specs=pl.BlockSpec((2,) + shape, lambda i: (0, 0, 0)),
        compiler_params=pltpu.CompilerParams(vmem_limit_bytes=VMEM_LIMIT),
        cost_estimate=pl.CostEstimate(flops=1_000_000, bytes_accessed=100_000, transcendentals=0),
    )(modulation, one, other)


def view_kernel(gain_ref, *refs):
    tokens, weights, (out_ref, h_ref, w_ref) = refs[:8], refs[8:12], refs[12:]
    rows = tokens[0].shape[0] * tokens[0].shape[1]
    for place, ref in enumerate(tokens):
        h_ref[place * rows : (place + 1) * rows, :] = ref[...].reshape(rows, ref.shape[-1])
    for part in range(3):
        for place, ref in enumerate(weights):
            w_ref[part, place * HS : (place + 1) * HS, :] = ref[part * HS : (part + 1) * HS, :]
    ones = head_sums()
    h = h_ref[...]
    query = lax.dot_general(h, w_ref[0], NT, preferred_element_type=F32)
    query = rms_norm(query, gain_ref[0:1] * HS ** (-0.5), ones)
    key = lax.dot_general(h, w_ref[1], NT, preferred_element_type=F32)
    key = rms_norm(key, gain_ref[1:2], ones).astype(BF)
    value = lax.dot_general(h, w_ref[2], NT, preferred_element_type=F32).astype(BF)
    out_ref[...] = attend(query, key, value, None, 1).reshape(out_ref.shape)


def view_attention(gains, tokens, weights):
    pair, toks, width = tokens[0].shape
    total = 8 * pair * toks
    return pl.pallas_call(
        view_kernel,
        out_shape=jax.ShapeDtypeStruct((Y, total // Y, LANES), BF),
        scratch_shapes=[pltpu.VMEM((total, width), BF), pltpu.VMEM((3, LANES, width), BF)],
        compiler_params=pltpu.CompilerParams(vmem_limit_bytes=VMEM_LIMIT),
        cost_estimate=pl.CostEstimate(
            flops=1_000_000, bytes_accessed=100_000, transcendentals=0
        ),
    )(gains, *tokens, *weights)


def join_kernel(gate_ref, mod_ref, keep_ref, got_ref, beside_ref, *refs):
    heads, pieces, outs, weight_ref = refs[:4], refs[4:8], refs[8:12], refs[12]
    for e in range(Y):
        for d, ref in enumerate(pieces):
            at = e * LANES + d * HS
            weight_ref[at : at + HS, :] = ref[e * HS : (e + 1) * HS, :]
    total = jnp.zeros((heads[0].shape[0], weight_ref.shape[-1]), F32)
    for e in range(Y):
        weight = weight_ref[e * LANES : (e + 1) * LANES, :]
        total = total + jnp.dot(heads[e][...], weight, preferred_element_type=F32)
    total = (total * gate_ref[0:1]).reshape((4,) + keep_ref.shape[1:])
    inputs = [keep_ref[0], got_ref[0], beside_ref[0], beside_ref[1]]
    for d in range(4):
        middle = (inputs[d].astype(F32) + total[d]).astype(BF)
        outs[d % 2][d // 2] = middle
        normed = layer_norm(middle.astype(F32), mod_ref[2:3], mod_ref[3:4])
        outs[2 + d % 2][d // 2] = normed.astype(BF)


def join_heads(gate, modulation, inputs, heads, pieces):
    pair, toks, width = inputs[0].shape
    return pl.pallas_call(
        join_kernel,
        out_shape=[jax.ShapeDtypeStruct((2, toks, width), BF)] * 4,
        scratch_shapes=[pltpu.VMEM((Y * LANES, width), BF)],
        compiler_params=pltpu.CompilerParams(vmem_limit_bytes=VMEM_LIMIT),
        cost_estimate=pl.CostEstimate(flops=1_000_000, bytes_accessed=100_000, transcendentals=0),
    )(gate, modulation, *inputs, *heads, *pieces)


def time_kernel(last, toks, place_ref, gain_ref, gate_ref, bias_ref, *refs):
    blocks, rest = refs[:3], refs[3:]
    extra, rest = (rest[:4], rest[4:]) if last else ((), rest)
    pieces, (out_ref, h_ref, q_ref, w_ref, o_ref, sems) = rest[:-6], rest[-6:]
    copies = []
    head = 0
    for piece in pieces:
        for part in range(piece.shape[0] // LANES):
            for kind in range(4):
                copy = pltpu.make_async_copy(
                    piece.at[pl.ds(part * LANES + kind * HS, HS), :],
                    w_ref.at[kind, pl.ds(head * HS, HS), :],
                    sems.at[head, kind],
                )
                copy.start()
                copies.append(copy)
            head += 1
    strips = toks // STRIP
    reach = 3 * 4 * STRIP
    for strip in range(strips):
        for place, ref in enumerate(blocks):
            for d in range(4):
                rows = ref[d, strip * STRIP : (strip + 1) * STRIP, :]
                at = strip * reach + (place * 4 + d) * STRIP
                h_ref[at : at + STRIP, :] = rows
                if place == 0:
                    at = (strip * 4 + d) * STRIP
                    q_ref[at : at + STRIP, :] = rows
    ones = head_sums()

    def heads_of(group):
        for copy in copies[group * GROUP * 4 : (group + 1) * GROUP * 4]:
            copy.wait()
        span = slice(group * LANES, (group + 1) * LANES)
        query = lax.dot_general(q_ref[...], w_ref[0, span, :], NT, preferred_element_type=F32)
        query = rms_norm(query, gain_ref[2:3] * HS ** (-0.5), ones)
        key = lax.dot_general(h_ref[...], w_ref[1, span, :], NT, preferred_element_type=F32)
        key = rms_norm(key, gain_ref[3:4], ones).astype(BF)
        value = lax.dot_general(h_ref[...], w_ref[2, span, :], NT, preferred_element_type=F32)
        return query, key, value.astype(BF)

    def attend_strips(group, query, key, value):
        for strip in range(strips):
            rows = slice(strip * 4 * STRIP, (strip + 1) * 4 * STRIP)
            sees = slice(strip * reach, (strip + 1) * reach)
            o_ref[rows, group * LANES : (group + 1) * LANES] = attend(
                query[rows], key[sees], value[sees], bias_ref[...], GROUP
            )

    held = heads_of(0)
    for group in range(1, head // GROUP):
        following = heads_of(group)
        attend_strips(group - 1, *held)
        held = following
    attend_strips(head // GROUP - 1, *held)
    branch = jnp.dot(o_ref[...], w_ref[3], preferred_element_type=F32)
    if not last:
        out_ref[...] = branch
        return
    partial_ref, even_ref, got_ref, beside_ref = extra
    branch = (branch + partial_ref[...]) * gate_ref[1:2]
    place = place_ref[0]
    middle = [(even_ref, 0), (got_ref, 0), (beside_ref, 0), (beside_ref, 1)]
    for d in range(4):
        ref, slot = middle[d]
        for strip in range(strips):
            rows = slice(strip * STRIP, (strip + 1) * STRIP)
            at = (strip * 4 + d) * STRIP
            out_ref[0, place ^ d, rows, :] = (
                ref[slot, rows, :].astype(F32) + branch[at : at + STRIP, :]
            ).astype(BF)


def time_attention(place, gains, gates, bias, blocks, pieces, extra=()):
    count, toks, width = blocks[0].shape
    own = count * toks
    heads = sum(piece.shape[0] for piece in pieces) // LANES
    vmem = pl.BlockSpec(memory_space=pltpu.VMEM)
    out_shape = jax.ShapeDtypeStruct((own, width), F32)
    if extra:
        out_shape = jax.ShapeDtypeStruct((1, count, toks, width), BF)
    return pl.pallas_call(
        functools.partial(time_kernel, bool(extra), toks),
        out_shape=out_shape,
        in_specs=[pl.BlockSpec(memory_space=pltpu.SMEM)]
        + [vmem] * (3 + len(blocks) + len(extra))
        + [pl.BlockSpec(memory_space=pl.ANY)] * len(pieces),
        out_specs=vmem,
        scratch_shapes=[
            pltpu.VMEM((3 * own, width), BF),
            pltpu.VMEM((own, width), BF),
            pltpu.VMEM((4, heads * HS, width), BF),
            pltpu.VMEM((own, heads * HS), BF),
            pltpu.SemaphoreType.DMA((heads, 4)),
        ],
        compiler_params=pltpu.CompilerParams(vmem_limit_bytes=VMEM_LIMIT),
        cost_estimate=pl.CostEstimate(
            flops=1_000_000, bytes_accessed=100_000, transcendentals=0
        ),
    )(place, gains, gates, bias, *blocks, *extra, *pieces)


def window_bias(place, first, frames, starts, toks):
    slots = jnp.arange(4, dtype=jnp.int32) ^ place
    low = starts[slots]
    frame = (first + 4 * jnp.array([0, -1, 1], jnp.int32)[:, None] + slots[None, :]).reshape(-1)
    allowed = (frame[None, :] >= low[:, None]) & (frame[None, :] < low[:, None] + WIN)
    allowed = allowed & (frame >= 0)[None, :] & (frame < frames)[None, :]
    same = jnp.eye(toks, dtype=bool)
    allowed = allowed[:, None, :, None] & same[None, :, None, :]
    return jnp.where(allowed, 0.0, -1e30).astype(F32).reshape(4 * toks, 12 * toks)


def on_device(
    frames_in, modulation, gates, qk_gain, view_qkv, view_out, time_qkv, time_out, window_start
):
    count, toks, width = frames_in.shape[1:]
    view = lax.axis_index("view")
    p = view % 4
    t = lax.axis_index("tm")
    steps = lax.axis_size("tm")
    gains = jnp.tile(qk_gain, (1, GROUP))

    def frames(*places):
        return jnp.stack(
            [lax.dynamic_index_in_dim(frames_in[0], p ^ d, 0, keepdims=False) for d in places]
        )

    parts = [view_out, hop(view_out, dy=-1), hop(view_out, dy=2), hop(view_out, dy=1)]
    time_own = jnp.concatenate([time_qkv.T, time_out], 0)

    keep, give = frames(0, 2), frames(1, 3)
    got = hop(give, dc=1)
    beside = hop(jnp.stack([keep[1], got[1]]), dx=1)
    first = norm_frames(modulation, keep, got)
    second = norm_frames(modulation, beside, beside)
    first, parts = fence(first, parts)
    back_a, ahead_a = hop(first, dy=1), hop(first, dy=-1)
    second, w_own = fence(second, view_qkv.T)
    w_x = hop(w_own, far=True)
    back_b, ahead_b = hop(second, dy=1), hop(second, dy=-1)
    far_a, far_b = hop(back_a, dy=1), hop(ahead_b, dy=-1)
    tokens = [first, second, ahead_a, ahead_b, far_a, far_b, back_a, back_b]
    heads_w = [w_own, hop(w_own, dc=1), w_x, hop(w_x, dc=1)]
    column = jnp.concatenate(fence(parts, ahead_a, back_a)[0], 0)
    column_x = hop(column, dx=1)
    tokens, heads_w, column, column_x, time_own = fence(
        tokens, heads_w, column, column_x, time_own
    )

    back_o, ahead_o = hop(time_own, dy=1), hop(time_own, dy=-1)
    time_x = hop(time_own, far=True)
    pieces0 = [column, hop(column, dc=1), column_x, hop(column_x, dc=1)]
    attended = view_attention(gains, tokens, heads_w)
    attended, pieces0 = fence(attended, pieces0)
    heads0 = [attended[0]] + [hop(attended[Y - e], dy=-e) for e in (1, 2, 3)]
    heads0, back_o, ahead_o = fence(heads0, back_o, ahead_o)

    back_x, ahead_x = hop(time_x, dy=1), hop(time_x, dy=-1)
    mine = [time_own, time_x]
    other = [hop(piece, dc=1) for piece in mine]
    even, odd, even_h, odd_h = join_heads(gates, modulation, [keep, got, beside], heads0, pieces0)

    got_h = hop(odd_h, dc=1)
    beside_h = hop(jnp.stack([even_h[1], got_h[1]]), dx=1)
    home = jnp.concatenate([even_h[:1], got_h[:1], beside_h], 0)
    home, odd, back_o, ahead_o, back_x, ahead_x, other = fence(
        home, odd, back_o, ahead_o, back_x, ahead_x, other
    )
    up = [(i, i + 1) for i in range(steps - 1)]
    before = lax.ppermute(home, "tm", up)
    behind = lax.ppermute(home, "tm", [(j, i) for i, j in up])
    far_o, far_x = hop(back_o, dy=1), hop(ahead_x, dy=-1)
    mine += [ahead_o, back_o, ahead_x, back_x]
    other += [hop(piece, dc=1) for piece in mine[2:]]
    got_m = hop(odd, dc=1)
    beside_m = hop(jnp.stack([even[1], got_m[1]]), dx=1)
    bias = window_bias(p, t * count, steps * count, window_start, STRIP)
    before, behind, mine, other, bias = fence(before, behind, mine, other, bias)
    place, blocks = p[None], [home, before, behind]
    partial = time_attention(place, gains, gates, bias, blocks, mine + other)
    partial, far_o, far_x, beside_m = fence(partial, far_o, far_x, beside_m)
    pieces2 = [far_o, far_x, hop(far_o, dc=1), hop(far_x, dc=1)]
    extra = [partial, even, got_m, beside_m]
    return time_attention(place, gains, gates, bias, blocks, pieces2, extra)


def solution(mesh):
    return jax.shard_map(
        on_device,
        mesh=mesh,
        in_specs=(
            P("view", "tm", None, None),
            P(),
            P(),
            P(),
            P(None, "view"),
            P("view", None),
            P(None, "view"),
            P("view", None),
            P("tm"),
        ),
        out_specs=P("view", "tm", None, None),
        check_vma=False,
    )
```

```python
import functools

import jax
import jax.numpy as jnp
from jax import lax
from jax.experimental import pallas as pl
from jax.experimental.pallas import tpu as pltpu
from jax.sharding import PartitionSpec as P

HS = 64
WIN = 8
EPSILON = 1e-06
GROUP = 4
STRIP = 16
LANES = GROUP * HS
BF = jnp.bfloat16
F32 = jnp.float32
NT = (((1,), (1,)), ((), ()))
VMEM_LIMIT = 56 * 1024 * 1024

Y, X, C = 4, 2, 2


def hop(value, dy=0, dx=0, dc=0, far=False):
    if far:
        steps = lax.axis_size("tm")
        pairs = []
        for view in range(Y * X * C):
            for step in range(steps):
                target = (view ^ C) * steps + (step + steps // 2) % steps
                pairs.append((view * steps + step, target))
        return lax.ppermute(value, ("view", "tm"), pairs)
    pairs = []
    for y in range(Y):
        for x in range(X):
            for c in range(C):
                source = (y * X + x) * C + c
                target = ((y + dy) % Y * X + (x ^ dx)) * C + (c ^ dc)
                pairs.append((source, target))
    return lax.ppermute(value, "view", pairs)


def fence(*values):
    return lax.optimization_barrier(values)


def layer_norm(inputs, shift_vec, scale_vec):
    average = jnp.mean(inputs, -1, keepdims=True)
    centred = inputs - average
    spread = jnp.mean(centred * centred, -1, keepdims=True)
    return centred * lax.rsqrt(spread + EPSILON) * (1.0 + scale_vec) + shift_vec


def head_sums():
    row = lax.broadcasted_iota(jnp.int32, (LANES, LANES), 0) // HS
    col = lax.broadcasted_iota(jnp.int32, (LANES, LANES), 1) // HS
    return (row == col).astype(F32).astype(BF)


def rms_norm(product, gain_row, ones):
    values = product.astype(BF).astype(F32)
    square = values * values
    upper = square.astype(BF)
    lower = (square - upper.astype(F32)).astype(BF)
    total = jnp.dot(upper, ones, preferred_element_type=F32)
    total = total + jnp.dot(lower, ones, preferred_element_type=F32)
    return values * lax.rsqrt(total * (1.0 / HS) + EPSILON) * gain_row


def attend(query, key, value, bias, stack):
    rows = query.shape[0]
    lane = lax.broadcasted_iota(jnp.int32, query.shape, 1) // HS
    result = jnp.zeros(query.shape, F32)
    for start in range(0, GROUP, stack):
        heads = range(start, start + stack)
        stacked = [jnp.where(lane == head, query, 0.0).astype(BF) for head in heads]
        stacked = jnp.concatenate(stacked, 0) if stack > 1 else stacked[0]
        scores = lax.dot_general(stacked, key, NT, preferred_element_type=F32)
        if bias is not None:
            scores = (scores.reshape(stack, rows, -1) + bias).reshape(stack * rows, -1)
        largest = jnp.max(scores, -1, keepdims=True)
        raised = jnp.exp(scores - largest)
        weights = (raised * (1.0 / jnp.sum(raised, -1, keepdims=True))).astype(BF)
        product = jnp.dot(weights, value, preferred_element_type=F32)
        for place, head in enumerate(heads):
            result = jnp.where(lane == head, product[place * rows : (place + 1) * rows], result)
    return result.astype(BF)


def norm_kernel(mod_ref, one_ref, other_ref, out_ref):
    for place, ref in enumerate((one_ref, other_ref)):
        out_ref[place] = layer_norm(ref[0].astype(F32), mod_ref[0:1], mod_ref[1:2]).astype(BF)


def norm_frames(modulation, one, other):
    shape = one.shape[1:]
    first = pl.BlockSpec((1,) + shape, lambda i: (0, 0, 0))
    second = pl.BlockSpec((1,) + shape, lambda i: (other.shape[0] - 1, 0, 0))
    if one is not other:
        second = first
    return pl.pallas_call(
        norm_kernel,
        grid=(1,),
        out_shape=jax.ShapeDtypeStruct((2,) + shape, BF),
        in_specs=[pl.BlockSpec(modulation.shape, lambda i: (0, 0)), first, second],
        out_specs=pl.BlockSpec((2,) + shape, lambda i: (0, 0, 0)),
        compiler_params=pltpu.CompilerParams(vmem_limit_bytes=VMEM_LIMIT),
        cost_estimate=pl.CostEstimate(flops=1_000_000, bytes_accessed=100_000, transcendentals=0),
    )(modulation, one, other)


def view_kernel(gain_ref, *refs):
    tokens, weights, outs, (h_ref, w_ref) = refs[:8], refs[8:12], refs[12:16], refs[16:]
    rows = tokens[0].shape[0] * tokens[0].shape[1]
    for place, ref in enumerate(tokens):
        h_ref[place * rows : (place + 1) * rows, :] = ref[...].reshape(rows, ref.shape[-1])
    for part in range(3):
        for place, ref in enumerate(weights):
            w_ref[part, place * HS : (place + 1) * HS, :] = ref[part * HS : (part + 1) * HS, :]
    ones = head_sums()
    h = h_ref[...]
    query = lax.dot_general(h, w_ref[0], NT, preferred_element_type=F32)
    query = rms_norm(query, gain_ref[0:1] * HS ** (-0.5), ones)
    key = lax.dot_general(h, w_ref[1], NT, preferred_element_type=F32)
    key = rms_norm(key, gain_ref[1:2], ones).astype(BF)
    value = lax.dot_general(h, w_ref[2], NT, preferred_element_type=F32).astype(BF)
    result = attend(query, key, value, None, 1)
    for e, ref in enumerate(outs):
        ref[...] = result[e * ref.shape[0] : (e + 1) * ref.shape[0]]


def view_attention(gains, tokens, weights):
    pair, toks, width = tokens[0].shape
    total = 8 * pair * toks
    return pl.pallas_call(
        view_kernel,
        out_shape=[jax.ShapeDtypeStruct((total // Y, LANES), BF)] * Y,
        scratch_shapes=[pltpu.VMEM((total, width), BF), pltpu.VMEM((3, LANES, width), BF)],
        compiler_params=pltpu.CompilerParams(vmem_limit_bytes=VMEM_LIMIT),
        cost_estimate=pl.CostEstimate(
            flops=1_000_000, bytes_accessed=100_000, transcendentals=0
        ),
    )(gains, *tokens, *weights)


def join_kernel(gate_ref, mod_ref, keep_ref, got_ref, beside_ref, *refs):
    heads, pieces, outs, weight_ref = refs[:4], refs[4:8], refs[8:12], refs[12]
    for e in range(Y):
        for d, ref in enumerate(pieces):
            at = e * LANES + d * HS
            weight_ref[at : at + HS, :] = ref[e * HS : (e + 1) * HS, :]
    total = jnp.zeros((heads[0].shape[0], weight_ref.shape[-1]), F32)
    for e in range(Y):
        weight = weight_ref[e * LANES : (e + 1) * LANES, :]
        total = total + jnp.dot(heads[e][...], weight, preferred_element_type=F32)
    total = (total * gate_ref[0:1]).reshape((4,) + keep_ref.shape[1:])
    inputs = [keep_ref[0], got_ref[0], beside_ref[0], beside_ref[1]]
    for d in range(4):
        middle = (inputs[d].astype(F32) + total[d]).astype(BF)
        outs[d % 2][d // 2] = middle
        normed = layer_norm(middle.astype(F32), mod_ref[2:3], mod_ref[3:4])
        outs[2 + d % 2][d // 2] = normed.astype(BF)


def join_heads(gate, modulation, inputs, heads, pieces):
    pair, toks, width = inputs[0].shape
    return pl.pallas_call(
        join_kernel,
        out_shape=[jax.ShapeDtypeStruct((2, toks, width), BF)] * 4,
        scratch_shapes=[pltpu.VMEM((Y * LANES, width), BF)],
        compiler_params=pltpu.CompilerParams(vmem_limit_bytes=VMEM_LIMIT),
        cost_estimate=pl.CostEstimate(flops=1_000_000, bytes_accessed=100_000, transcendentals=0),
    )(gate, modulation, *inputs, *heads, *pieces)


def time_kernel(last, toks, place_ref, gain_ref, gate_ref, bias_ref, *refs):
    blocks, rest = refs[:3], refs[3:]
    extra, rest = (rest[:4], rest[4:]) if last else ((), rest)
    pieces, (out_ref, h_ref, q_ref, w_ref, o_ref, sems) = rest[:-6], rest[-6:]
    copies = []
    head = 0
    for piece in pieces:
        for part in range(piece.shape[0] // LANES):
            for kind in range(4):
                copy = pltpu.make_async_copy(
                    piece.at[pl.ds(part * LANES + kind * HS, HS), :],
                    w_ref.at[kind, pl.ds(head * HS, HS), :],
                    sems.at[head, kind],
                )
                copy.start()
                copies.append(copy)
            head += 1
    strips = toks // STRIP
    reach = 3 * 4 * STRIP
    for strip in range(strips):
        for place, ref in enumerate(blocks):
            for d in range(4):
                rows = ref[d, strip * STRIP : (strip + 1) * STRIP, :]
                at = strip * reach + (place * 4 + d) * STRIP
                h_ref[at : at + STRIP, :] = rows
                if place == 0:
                    at = (strip * 4 + d) * STRIP
                    q_ref[at : at + STRIP, :] = rows
    ones = head_sums()

    def heads_of(group):
        for copy in copies[group * GROUP * 4 : (group + 1) * GROUP * 4]:
            copy.wait()
        span = slice(group * LANES, (group + 1) * LANES)
        query = lax.dot_general(q_ref[...], w_ref[0, span, :], NT, preferred_element_type=F32)
        query = rms_norm(query, gain_ref[2:3] * HS ** (-0.5), ones)
        key = lax.dot_general(h_ref[...], w_ref[1, span, :], NT, preferred_element_type=F32)
        key = rms_norm(key, gain_ref[3:4], ones).astype(BF)
        value = lax.dot_general(h_ref[...], w_ref[2, span, :], NT, preferred_element_type=F32)
        return query, key, value.astype(BF)

    def attend_strips(group, query, key, value):
        for strip in range(strips):
            rows = slice(strip * 4 * STRIP, (strip + 1) * 4 * STRIP)
            sees = slice(strip * reach, (strip + 1) * reach)
            o_ref[rows, group * LANES : (group + 1) * LANES] = attend(
                query[rows], key[sees], value[sees], bias_ref[...], GROUP
            )

    held = heads_of(0)
    for group in range(1, head // GROUP):
        following = heads_of(group)
        attend_strips(group - 1, *held)
        held = following
    attend_strips(head // GROUP - 1, *held)
    branch = jnp.dot(o_ref[...], w_ref[3], preferred_element_type=F32)
    if not last:
        out_ref[...] = branch
        return
    partial_ref, even_ref, got_ref, beside_ref = extra
    branch = (branch + partial_ref[...]) * gate_ref[1:2]
    place = place_ref[0]
    middle = [(even_ref, 0), (got_ref, 0), (beside_ref, 0), (beside_ref, 1)]
    for d in range(4):
        ref, slot = middle[d]
        for strip in range(strips):
            rows = slice(strip * STRIP, (strip + 1) * STRIP)
            at = (strip * 4 + d) * STRIP
            out_ref[0, place ^ d, rows, :] = (
                ref[slot, rows, :].astype(F32) + branch[at : at + STRIP, :]
            ).astype(BF)


def time_attention(place, gains, gates, bias, blocks, pieces, extra=()):
    count, toks, width = blocks[0].shape
    own = count * toks
    heads = sum(piece.shape[0] for piece in pieces) // LANES
    vmem = pl.BlockSpec(memory_space=pltpu.VMEM)
    out_shape = jax.ShapeDtypeStruct((own, width), F32)
    if extra:
        out_shape = jax.ShapeDtypeStruct((1, count, toks, width), BF)
    return pl.pallas_call(
        functools.partial(time_kernel, bool(extra), toks),
        out_shape=out_shape,
        in_specs=[pl.BlockSpec(memory_space=pltpu.SMEM)]
        + [vmem] * (3 + len(blocks) + len(extra))
        + [pl.BlockSpec(memory_space=pl.ANY)] * len(pieces),
        out_specs=vmem,
        scratch_shapes=[
            pltpu.VMEM((3 * own, width), BF),
            pltpu.VMEM((own, width), BF),
            pltpu.VMEM((4, heads * HS, width), BF),
            pltpu.VMEM((own, heads * HS), BF),
            pltpu.SemaphoreType.DMA((heads, 4)),
        ],
        compiler_params=pltpu.CompilerParams(vmem_limit_bytes=VMEM_LIMIT),
        cost_estimate=pl.CostEstimate(flops=8000000000, bytes_accessed=16000000, transcendentals=0),
    )(place, gains, gates, bias, *blocks, *extra, *pieces)


def window_bias(place, first, frames, starts, toks):
    slots = jnp.arange(4, dtype=jnp.int32) ^ place
    low = starts[slots]
    frame = (first + 4 * jnp.array([0, -1, 1], jnp.int32)[:, None] + slots[None, :]).reshape(-1)
    allowed = (frame[None, :] >= low[:, None]) & (frame[None, :] < low[:, None] + WIN)
    allowed = allowed & (frame >= 0)[None, :] & (frame < frames)[None, :]
    same = jnp.eye(toks, dtype=bool)
    allowed = allowed[:, None, :, None] & same[None, :, None, :]
    return jnp.where(allowed, 0.0, -1e30).astype(F32).reshape(4 * toks, 12 * toks)


def on_device(
    frames_in, modulation, gates, qk_gain, view_qkv, view_out, time_qkv, time_out, window_start
):
    count, toks, width = frames_in.shape[1:]
    view = lax.axis_index("view")
    p = view % 4
    t = lax.axis_index("tm")
    steps = lax.axis_size("tm")
    gains = jnp.tile(qk_gain, (1, GROUP))

    def frames(*places):
        return jnp.stack(
            [lax.dynamic_index_in_dim(frames_in[0], p ^ d, 0, keepdims=False) for d in places]
        )

    parts = [view_out, hop(view_out, dy=-1), hop(view_out, dy=2), hop(view_out, dy=1)]
    time_own = jnp.concatenate([time_qkv.T, time_out], 0)

    keep, give = frames(0, 2), frames(1, 3)
    got = hop(give, dc=1)
    beside = hop(jnp.stack([keep[1], got[1]]), dx=1)
    first = norm_frames(modulation, keep, got)
    second = norm_frames(modulation, beside, beside)
    bias = window_bias(p, t * count, steps * count, window_start, STRIP)
    first, parts, gains, bias = fence(first, parts, gains, bias)
    back_a, ahead_a = hop(first, dy=1), hop(first, dy=-1)
    second, w_own = fence(second, view_qkv.T)
    w_x = hop(w_own, far=True)
    back_b, ahead_b = hop(second, dy=1), hop(second, dy=-1)
    far_a, far_b = hop(back_a, dy=1), hop(ahead_b, dy=-1)
    tokens = [first, second, ahead_a, ahead_b, far_a, far_b, back_a, back_b]
    heads_w = [w_own, hop(w_own, dc=1), w_x, hop(w_x, dc=1)]
    column = jnp.concatenate(fence(parts, ahead_a, back_a)[0], 0)
    column_x = hop(column, dx=1)
    tokens, heads_w, column, column_x, time_own = fence(
        tokens, heads_w, column, column_x, time_own
    )

    back_o, ahead_o = hop(time_own, dy=1), hop(time_own, dy=-1)
    time_x = hop(time_own, far=True)
    pieces0 = [column, hop(column, dc=1), column_x, hop(column_x, dc=1)]
    attended = view_attention(gains, tokens, heads_w)
    attended, pieces0 = fence(attended, pieces0)
    heads0 = [attended[0]] + [hop(attended[Y - e], dy=-e) for e in (1, 2, 3)]
    heads0, back_o, ahead_o = fence(heads0, back_o, ahead_o)

    back_x, ahead_x = hop(time_x, dy=1), hop(time_x, dy=-1)
    mine = [time_own, time_x]
    other = [hop(piece, dc=1) for piece in mine]
    even, odd, even_h, odd_h = join_heads(gates, modulation, [keep, got, beside], heads0, pieces0)

    got_h = hop(odd_h, dc=1)
    beside_h = hop(jnp.stack([even_h[1], got_h[1]]), dx=1)
    home = jnp.concatenate([even_h[:1], got_h[:1], beside_h], 0)
    home, odd, back_o, ahead_o, back_x, ahead_x, other = fence(
        home, odd, back_o, ahead_o, back_x, ahead_x, other
    )
    up = [(i, i + 1) for i in range(steps - 1)]
    before = lax.ppermute(home, "tm", up)
    behind = lax.ppermute(home, "tm", [(j, i) for i, j in up])
    far_o, far_x = hop(back_o, dy=1), hop(ahead_x, dy=-1)
    mine += [ahead_o, back_o, ahead_x, back_x]
    other += [hop(piece, dc=1) for piece in mine[2:]]
    got_m = hop(odd, dc=1)
    beside_m = hop(jnp.stack([even[1], got_m[1]]), dx=1)
    before, behind, mine, other = fence(before, behind, mine, other)
    place, blocks = p[None], [home, before, behind]
    partial = time_attention(place, gains, gates, bias, blocks, mine + other)
    partial, far_o, far_x, beside_m = fence(partial, far_o, far_x, beside_m)
    pieces2 = [far_o, far_x, hop(far_o, dc=1), hop(far_x, dc=1)]
    extra = [partial, even, got_m, beside_m]
    return time_attention(place, gains, gates, bias, blocks, pieces2, extra)


def solution(mesh):
    return jax.shard_map(
        on_device,
        mesh=mesh,
        in_specs=(
            P("view", "tm", None, None),
            P(),
            P(),
            P(),
            P(None, "view"),
            P("view", None),
            P(None, "view"),
            P("view", None),
            P("tm"),
        ),
        out_specs=P("view", "tm", None, None),
        check_vma=False,
    )
```
